32 devices in a mesh: chan: 8 (over z, y), win: 4 (over x, core).
Axes of the slice: x: 2, y: 2, z: 4, core: 2. Of those that a mesh axis runs over, the one named last changes fastest.
Arguments:
- spec_re: bfloat16 [8, 128, 5120], P(None, 'win', 'chan'), may hold values from -6 to 6
- spec_im: bfloat16 [8, 128, 5120], P(None, 'win', 'chan'), may hold values from -6 to 6
- valid: int32 [128, 5120], P('win', 'chan'), may hold values from 0 to 1, as said below
Outputs:
- stack_re: float32 [8, 5120, 5120], P(None, 'chan', 'win')
- stack_im: float32 [8, 5120, 5120], P(None, 'chan', 'win')
The draws below stay inside these ranges and needn't reach their ends.
Inputs may be any that keep to these rules, and one draw needn't show every extreme that they name: `valid`: each entry is 0 or 1; some channels are 0 in every window.
All inputs are finite; a program needn't handle non-finite values.
Results may differ from the reference program's by a relative error of at most 0.012.
Values may be sent and summed in bfloat16 or wider, within the bound.
A program may use at most 384 MiB of HBM per device.

```python
import jax
import jax.numpy as jnp
from jax import lax

C = 5120
F = 8
W_DEV = 32
WINDOWS = 128
N_WIN = 4


def draw_valid(key, part):
    key = jax.random.fold_in(key, 11)
    dead_key, keep_key = jax.random.split(key)
    dead = jax.random.randint(dead_key, (C,), 0, 32) == 0
    keep = jax.random.randint(keep_key, (WINDOWS, C), 0, 20) >= 3
    return jnp.where(dead[None, :], 0, keep.astype(jnp.int32)).astype(jnp.int32)


def level_of(key, shape, shards, least, high):
    def one(position, shards_of):
        draws = jax.random.uniform(jax.random.fold_in(jax.random.fold_in(key, 6), position), (shards_of,), jnp.float32, least / len(shards), high / len(shards))
        return jnp.repeat(jnp.exp(draws), shape[position] // shards_of).reshape((-1,) + (1,) * (len(shape) - position - 1))

    loudness = one(*shards[0])
    for cut in shards[1:]:
        loudness = loudness * one(*cut)
    return loudness


def noise(own_key, shape, width, most, pieces=(), held_as=jnp.bfloat16):
    entries = width * jax.random.normal(own_key, shape, jnp.float32)
    if pieces:
        entries = entries * level_of(own_key, shape, pieces, -0.22, 0.18)
    return jnp.clip(entries, -most, most).astype(held_as)


def setup_inputs(seed: int = 0) -> dict:
    seeds = jax.random.split(jax.random.key(seed), 4)
    return {
        "spec_re": noise(seeds[0], (F, WINDOWS, C), 1.0, 6.0, ((1, 4), (2, 8))),
        "spec_im": noise(seeds[1], (F, WINDOWS, C), 1.0, 6.0, ((1, 4), (2, 8))),
        "valid": draw_valid(jax.random.fold_in(seeds[3], 71), 0),
    }


water_level = 1.0

def reference(spec_re, spec_im, valid):
    mask = valid.astype(jnp.float32)
    real_part = spec_re.astype(jnp.float32)
    imag_part = spec_im.astype(jnp.float32)
    amp = jnp.sqrt(real_part * real_part + imag_part * imag_part)
    factor = mask[None] / jnp.maximum(amp, water_level)
    white_re = (real_part * factor).astype(jnp.bfloat16)
    white_im = (imag_part * factor).astype(jnp.bfloat16)
    count = jnp.dot(mask.T, mask, precision=lax.Precision.HIGHEST)

    def per_bin(pair):
        bin_re, bin_im = pair
        total = jnp.zeros((2 * C, C), jnp.float32)
        for group in range(N_WIN):
            left_re = bin_re[group * W_DEV:(group + 1) * W_DEV]
            left_im = bin_im[group * W_DEV:(group + 1) * W_DEV]
            right = jnp.concatenate([left_re, left_im], 0)
            left = jnp.concatenate([right, jnp.concatenate([left_im, -left_re], 0)], 1)
            product = jnp.dot(left.T, right, preferred_element_type=jnp.float32)
            rounded = lax.optimization_barrier(product.astype(jnp.bfloat16))
            total = total + rounded.astype(jnp.float32)
        return (total[:C], total[C:])
    total_re, total_im = lax.map(per_bin, (white_re, white_im))
    denom = jnp.maximum(count, 1.0)[None]
    return (total_re / denom, total_im / denom)
```

```python
import functools

import jax
import jax.numpy as jnp
from jax import lax
from jax.experimental import pallas as pl
from jax.experimental.pallas import tpu as pltpu
from jax.sharding import PartitionSpec as P

water_level = 1.0
MESH = pl.DeviceIdType.MESH


def whitened(real_part, imag_part, mask):
    real_part = real_part.astype(jnp.float32)
    imag_part = imag_part.astype(jnp.float32)
    power = real_part * real_part + imag_part * imag_part
    factor = mask * lax.rsqrt(jnp.maximum(power, water_level * water_level))
    return (real_part * factor).astype(jnp.bfloat16), (imag_part * factor).astype(jnp.bfloat16)


def gather_kernel(bins, wins, pieces, planes,
                  re_ref, im_ref, valid_ref, rows, cols, relay, own,
                  core_s, core_r, xrow_s, xrow_r, pair_s, pair_r,
                  up_p, dn_p, zp_r, up_q, dn_q, zq_r, x_s, x_r, y_s, y_r, local_s):
    c = lax.axis_index("chan")
    w = lax.axis_index("win")
    z, y = c // 2, c % 2
    core = w % 2
    plane, other = w, (w + 2) % 4
    mate = w + 1 - 2 * core
    s0 = (w, mate)
    s1 = ((w + 2) % 4, (mate + 2) % 4)
    dev_core = (c, mate)
    dev_x = (c, (w + 2) % 4)
    dev_y = (c + 1 - 2 * y, w)
    dev_up = (jnp.minimum(c + 2, 2 * planes - 1), w)
    dev_dn = (jnp.maximum(c - 2, 0), w)
    has_up, has_dn = z < planes - 1, z > 0

    barrier = pltpu.get_barrier_semaphore()
    for dev in (dev_core, dev_x, dev_y):
        pl.semaphore_signal(barrier, inc=1, device_id=dev, device_id_type=MESH)

    @pl.when(has_up)
    def _():
        pl.semaphore_signal(barrier, inc=1, device_id=dev_up, device_id_type=MESH)

    @pl.when(has_dn)
    def _():
        pl.semaphore_signal(barrier, inc=1, device_id=dev_dn, device_id_type=MESH)

    peers = 3 + has_up.astype(jnp.int32) + has_dn.astype(jnp.int32)
    pl.semaphore_wait(barrier, peers)

    depth = 2 * wins
    per = bins // pieces
    cuts = []
    for i in range(pieces):
        size = per * depth + (wins if i == pieces - 1 else 0)
        cuts.append(pl.ds(i * per * depth, size))

    sent = []

    def send(src, dst, ssem, rsem, dev, cond=None):
        def make():
            return pltpu.make_async_remote_copy(
                src_ref=src, dst_ref=dst, send_sem=ssem, recv_sem=rsem,
                device_id=dev, device_id_type=MESH)
        if cond is None:
            make().start()
        else:
            @pl.when(cond)
            def _():
                make().start()
        sent.append((make, cond))

    def arrive(dst, ssem, rsem):
        pltpu.make_async_remote_copy(
            src_ref=dst, dst_ref=dst, send_sem=ssem, recv_sem=rsem,
            device_id=dev_core, device_id_type=MESH).wait_recv()

    is_p, is_q = z == plane, z == other
    go_up_p = (z >= plane) & has_up
    go_dn_p = (z <= plane) & has_dn
    go_up_q = (z >= other) & has_up
    go_dn_q = (z <= other) & has_dn

    def along(i, u, kk, src, cond_at, into_p):
        cut = cuts[i]
        if into_p:
            dst = cols.at[y, s0[kk], cut]
            send(src, dst, up_p.at[u], zp_r.at[u], dev_up, cond_at & go_up_p)
            send(src, dst, dn_p.at[u], zp_r.at[u], dev_dn, cond_at & go_dn_p)
        else:
            dst = relay.at[kk, cut]
            send(src, dst, up_q.at[u], zq_r.at[u], dev_up, cond_at & go_up_q)
            send(src, dst, dn_q.at[u], zq_r.at[u], dev_dn, cond_at & go_dn_q)

    def source(i, kk, src):
        u = kk * pieces + i
        along(i, u, kk, src, is_p, True)
        along(i, u, kk, src, is_q, False)
        send(src, cols.at[y, s0[kk], cuts[i]], y_s.at[u], y_r.at[u], dev_y, is_p)

    mask = valid_ref[...].astype(jnp.float32)
    locals_ = []
    for i in range(pieces):
        for f in range(i * per, (i + 1) * per):
            wr, wi = whitened(re_ref[f], im_ref[f], mask)
            own[pl.ds(f * depth, wins), :] = wr
            own[pl.ds(f * depth + wins, wins), :] = wi
        if i == pieces - 1:
            own[pl.ds(bins * depth, wins), :] = mask.astype(jnp.bfloat16)
        src = own.at[cuts[i]]
        send(src, rows.at[w, cuts[i]], core_s.at[i], core_r.at[i], dev_core)
        source(i, 0, src)
        send(src, rows.at[w, cuts[i]], xrow_s.at[i], xrow_r.at[i], dev_x)
        copy = pltpu.make_async_copy(src, rows.at[w, cuts[i]], local_s.at[i])
        copy.start()
        locals_.append(copy)

    half = 2 * pieces
    for kk in range(2):
        for i in range(pieces):
            cut = cuts[i]
            u = kk * pieces + i
            if kk == 0:
                arrive(rows.at[mate, cut], core_s.at[i], core_r.at[i])
                source(i, 1, rows.at[mate, cut])

            @pl.when(jnp.logical_not(is_p))
            def _():
                arrive(cols.at[y, s0[kk], cut], up_p.at[u], zp_r.at[u])

            here = cols.at[y, s0[kk], cut]
            along(i, u, kk, here, jnp.logical_not(is_p), True)
            send(here, here, y_s.at[u], y_r.at[u], dev_y, jnp.logical_not(is_p))

            @pl.when(jnp.logical_not(is_q))
            def _():
                arrive(relay.at[kk, cut], up_q.at[u], zq_r.at[u])

            here = relay.at[kk, cut]
            along(i, u, kk, here, jnp.logical_not(is_q), False)
            send(here, cols.at[y, s0[kk], cut], x_s.at[u], x_r.at[u], dev_x, jnp.logical_not(is_q))

            here = rows.at[s1[kk], cut]
            if kk == 0:
                arrive(here, xrow_s.at[i], xrow_r.at[i])
                send(here, here, pair_s.at[i], pair_r.at[i], dev_core)
            else:
                arrive(here, pair_s.at[i], pair_r.at[i])
            send(here, cols.at[y, s1[kk], cut], y_s.at[half + u], y_r.at[half + u], dev_y, is_p)

            @pl.when(jnp.logical_not(is_p))
            def _():
                arrive(cols.at[y, s1[kk], cut], x_s.at[u], x_r.at[u])

            here = cols.at[y, s1[kk], cut]
            send(here, here, y_s.at[half + u], y_r.at[half + u], dev_y, jnp.logical_not(is_p))

    for copy in locals_:
        copy.wait()

    @pl.when(is_p)
    def _():
        copy = pltpu.make_async_copy(rows, cols.at[y], local_s.at[pieces])
        copy.start()
        copy.wait()

    for kk in range(2):
        for i in range(pieces):
            u = kk * pieces + i
            arrive(cols.at[1 - y, s0[kk], cuts[i]], y_s.at[u], y_r.at[u])
            arrive(cols.at[1 - y, s1[kk], cuts[i]], y_s.at[half + u], y_r.at[half + u])

    for make, cond in sent:
        if cond is None:
            make().wait_send()
        else:
            @pl.when(cond)
            def _(make=make):
                make().wait_send()


def gather_call(spec_re, spec_im, valid, planes):
    bins, wins, width = spec_re.shape
    pieces = 4
    deep = bins * 2 * wins + wins
    sems = lambda n: pltpu.SemaphoreType.DMA((n,))
    u = 2 * pieces
    return pl.pallas_call(
        functools.partial(gather_kernel, bins, wins, pieces, planes),
        out_shape=[
            jax.ShapeDtypeStruct((4, deep, width), jnp.bfloat16),
            jax.ShapeDtypeStruct((2, 4, deep, width), jnp.bfloat16),
            jax.ShapeDtypeStruct((2, deep, width), jnp.bfloat16),
        ],
        in_specs=[pl.BlockSpec(memory_space=pltpu.VMEM)] * 3,
        out_specs=[pl.BlockSpec(memory_space=pl.ANY)] * 3,
        scratch_shapes=[
            pltpu.VMEM((deep, width), jnp.bfloat16),
            sems(pieces), sems(pieces), sems(pieces), sems(pieces), sems(pieces), sems(pieces),
            sems(u), sems(u), sems(u), sems(u), sems(u), sems(u),
            sems(u), sems(u), sems(2 * u), sems(2 * u), sems(pieces + 1),
        ],
        compiler_params=pltpu.CompilerParams(
            collective_id=0, has_side_effects=True, vmem_limit_bytes=16 * 2**20),
    )(spec_re, spec_im, valid)


def spectra_kernel(row_ref, row_mask_ref, col_ref, col_mask_ref, re_ref, im_ref, left_re, left_im, scale):
    f, h = pl.program_id(0), pl.program_id(1)
    wins = row_mask_ref.shape[1]
    width = row_ref.shape[2]
    groups = row_ref.shape[0]

    @pl.when(h == 0)
    def _():
        block = row_ref[...]
        real_part, imag_part = block[:, :wins], block[:, wins:]
        depth = groups * 2 * wins
        left_re[...] = block.reshape(depth, width).T
        left_im[...] = jnp.concatenate([imag_part, -real_part], 1).reshape(depth, width).T

    @pl.when(f == 0)
    def _():
        rows_mask = row_mask_ref[...].reshape(groups * wins, width)
        cols_mask = col_mask_ref[0].reshape(groups * wins, width)
        count = lax.dot_general(rows_mask, cols_mask, (((0,), (0,)), ((), ())),
                                preferred_element_type=jnp.float32)
        scale[h] = 1.0 / jnp.maximum(count, 1.0)

    right = col_ref[0].reshape(groups * 2 * wins, width)
    re_ref[0] = jnp.dot(left_re[...], right, preferred_element_type=jnp.float32) * scale[h]
    im_ref[0] = jnp.dot(left_im[...], right, preferred_element_type=jnp.float32) * scale[h]


def spectra_call(rows, cols, bins, wins):
    groups, _, width = rows.shape
    halves = cols.shape[0]
    depth = groups * 2 * wins
    out = jax.ShapeDtypeStruct((bins, width, halves * width), jnp.float32)
    last = 2 * bins
    return pl.pallas_call(
        spectra_kernel,
        grid=(bins, halves),
        out_shape=[out, out],
        in_specs=[
            pl.BlockSpec((groups, 2 * wins, width), lambda f, h: (0, f, 0)),
            pl.BlockSpec((groups, wins, width), lambda f, h: (0, last, 0)),
            pl.BlockSpec((1, groups, 2 * wins, width), lambda f, h: (h, 0, f, 0)),
            pl.BlockSpec((1, groups, wins, width), lambda f, h: (h, 0, last, 0)),
        ],
        out_specs=[pl.BlockSpec((1, width, width), lambda f, h: (f, 0, h))] * 2,
        scratch_shapes=[
            pltpu.VMEM((width, depth), jnp.bfloat16),
            pltpu.VMEM((width, depth), jnp.bfloat16),
            pltpu.VMEM((halves, width, width), jnp.float32),
        ],
        compiler_params=pltpu.CompilerParams(vmem_limit_bytes=28 * 2**20),
    )(rows, rows, cols, cols)


def on_device_kernels(spec_re, spec_im, valid):
    bins, wins, _ = spec_re.shape
    rows, cols, _ = gather_call(spec_re, spec_im, valid, lax.axis_size("chan") // 2)
    return tuple(spectra_call(rows, cols, bins, wins))


def on_device_general(spec_re, spec_im, valid):
    bins, wins, width = spec_re.shape
    mask = valid.astype(jnp.float32)
    white_re, white_im = whitened(spec_re, spec_im, mask[None])
    mine = jnp.concatenate(
        [white_re.reshape(bins * wins, width), white_im.reshape(bins * wins, width),
         mask.astype(jnp.bfloat16)], 0)
    rows = lax.all_gather(mine, "win")
    groups = rows.shape[0]
    every = lax.all_gather(rows, "chan")
    blocks = every.shape[0] // groups
    cols = lax.dynamic_slice_in_dim(every, lax.axis_index("win") * blocks, blocks, 0)
    cols = jnp.transpose(cols, (1, 2, 0, 3)).reshape(groups, rows.shape[1], blocks * width)

    def split(array):
        n = array.shape[2]
        size = bins * wins
        return (array[:, :size].reshape(groups, bins, wins, n),
                array[:, size:2 * size].reshape(groups, bins, wins, n), array[:, 2 * size:])

    row_re, row_im, row_mask = split(rows)
    col_re, col_im, col_mask = split(cols)
    right = jnp.concatenate([col_re, col_im], 2)

    def product(left):
        return jnp.einsum("gfwi,gfwj->fij", left, right, preferred_element_type=jnp.float32)

    count = jnp.einsum("gwi,gwj->ij", row_mask, col_mask, preferred_element_type=jnp.float32)
    denom = jnp.maximum(count, 1.0)[None]
    total_re = product(jnp.concatenate([row_re, row_im], 2))
    total_im = product(jnp.concatenate([row_im, -row_re], 2))
    return (total_re / denom, total_im / denom)


def solution(mesh):
    fits = mesh.shape["chan"] == 8 and mesh.shape["win"] == 4
    on_device = on_device_kernels if fits else on_device_general
    in_specs = (P(None, "win", "chan"), P(None, "win", "chan"), P("win", "chan"))
    out_specs = (P(None, "chan", "win"), P(None, "chan", "win"))
    return jax.shard_map(
        on_device, mesh=mesh, in_specs=in_specs, out_specs=out_specs, check_vma=False
    )
```

```python
import functools

import jax
import jax.numpy as jnp
from jax import lax
from jax.experimental import pallas as pl
from jax.experimental.pallas import tpu as pltpu
from jax.sharding import PartitionSpec as P

water_level = 1.0
MESH = pl.DeviceIdType.MESH


def whitened(real_part, imag_part, mask):
    real_part = real_part.astype(jnp.float32)
    imag_part = imag_part.astype(jnp.float32)
    power = real_part * real_part + imag_part * imag_part
    factor = mask * lax.rsqrt(jnp.maximum(power, water_level * water_level))
    return (real_part * factor).astype(jnp.bfloat16), (imag_part * factor).astype(jnp.bfloat16)


def gather_kernel(bins, wins, pieces, planes,
                  re_hbm, im_hbm, valid_hbm, rows, cols, relay, re_ref, im_ref, valid_ref, own, input_s,
                  core_s, core_r, xrow_s, xrow_r, pair_s, pair_r,
                  up_p, dn_p, zp_r, up_q, dn_q, zq_r, x_s, x_r, y_s, y_r, local_s):
    c = lax.axis_index("chan")
    w = lax.axis_index("win")
    z, y = c // 2, c % 2
    core = w % 2
    plane, other = w, (w + 2) % 4
    mate = w + 1 - 2 * core
    s0 = (w, mate)
    s1 = ((w + 2) % 4, (mate + 2) % 4)
    dev_core = (c, mate)
    dev_x = (c, (w + 2) % 4)
    dev_y = (c + 1 - 2 * y, w)
    dev_up = (jnp.minimum(c + 2, 2 * planes - 1), w)
    dev_dn = (jnp.maximum(c - 2, 0), w)
    has_up, has_dn = z < planes - 1, z > 0

    loads = [pltpu.make_async_copy(src, dst, input_s.at[n]) for n, (src, dst) in enumerate(
        ((re_hbm, re_ref), (im_hbm, im_ref), (valid_hbm, valid_ref)))]
    for load in loads:
        load.start()

    barrier = pltpu.get_barrier_semaphore()
    for dev in (dev_core, dev_x, dev_y):
        pl.semaphore_signal(barrier, inc=1, device_id=dev, device_id_type=MESH)

    @pl.when(has_up)
    def _():
        pl.semaphore_signal(barrier, inc=1, device_id=dev_up, device_id_type=MESH)

    @pl.when(has_dn)
    def _():
        pl.semaphore_signal(barrier, inc=1, device_id=dev_dn, device_id_type=MESH)

    peers = 3 + has_up.astype(jnp.int32) + has_dn.astype(jnp.int32)
    pl.semaphore_wait(barrier, peers)

    depth = 2 * wins
    per = bins // pieces
    cuts = []
    for i in range(pieces):
        size = per * depth + (wins if i == pieces - 1 else 0)
        cuts.append(pl.ds(i * per * depth, size))

    sent = []

    def send(src, dst, ssem, rsem, dev, cond=None):
        def make():
            return pltpu.make_async_remote_copy(
                src_ref=src, dst_ref=dst, send_sem=ssem, recv_sem=rsem,
                device_id=dev, device_id_type=MESH)
        if cond is None:
            make().start()
        else:
            @pl.when(cond)
            def _():
                make().start()
        sent.append((make, cond))

    def settle(first, last):
        for n in range(first, last):
            if sent[n] is not None:
                make, cond = sent[n]

                @pl.when(cond)
                def _():
                    make().wait_send()

                sent[n] = None

    def arrive(dst, ssem, rsem):
        pltpu.make_async_remote_copy(
            src_ref=dst, dst_ref=dst, send_sem=ssem, recv_sem=rsem,
            device_id=dev_core, device_id_type=MESH).wait_recv()

    is_p, is_q = z == plane, z == other
    go_up_p = (z >= plane) & has_up
    go_dn_p = (z <= plane) & has_dn
    go_up_q = (z >= other) & has_up
    go_dn_q = (z <= other) & has_dn

    def along(i, u, kk, src, cond_at, into_p):
        cut = cuts[i]
        if into_p:
            dst = cols.at[y, s0[kk], cut]
            send(src, dst, up_p.at[u], zp_r.at[u], dev_up, cond_at & go_up_p)
            send(src, dst, dn_p.at[u], zp_r.at[u], dev_dn, cond_at & go_dn_p)
        else:
            dst = relay.at[kk, cut]
            send(src, dst, up_q.at[u], zq_r.at[u], dev_up, cond_at & go_up_q)
            send(src, dst, dn_q.at[u], zq_r.at[u], dev_dn, cond_at & go_dn_q)

    late_up, late_dn = z == planes - 2, z == 1

    def source_z(i, kk, src, late):
        u = kk * pieces + i
        cut = cuts[i]
        to_up = has_up & (late_up if late else jnp.logical_not(late_up))
        to_dn = has_dn & (late_dn if late else jnp.logical_not(late_dn))
        dst = cols.at[y, s0[kk], cut]
        send(src, dst, up_p.at[u], zp_r.at[u], dev_up, is_p & to_up)
        send(src, dst, dn_p.at[u], zp_r.at[u], dev_dn, is_p & to_dn)
        dst = relay.at[kk, cut]
        send(src, dst, up_q.at[u], zq_r.at[u], dev_up, is_q & to_up)
        send(src, dst, dn_q.at[u], zq_r.at[u], dev_dn, is_q & to_dn)

    def source(i, kk, src):
        u = kk * pieces + i
        source_z(i, kk, src, False)
        send(src, cols.at[y, s0[kk], cuts[i]], y_s.at[u], y_r.at[u], dev_y, is_p)

    rows_first_out = (z // 2) == 1 - w // 2
    rows_first_in = (z // 2) == w // 2

    for load in loads:
        load.wait()
    mask = valid_ref[...].astype(jnp.float32)
    locals_ = []
    marks = []
    lag = 1
    for i in range(pieces):
        for f in range(i * per, (i + 1) * per):
            wr, wi = whitened(re_ref[f], im_ref[f], mask)
            own[pl.ds(f * depth, wins), :] = wr
            own[pl.ds(f * depth + wins, wins), :] = wi
        if i == pieces - 1:
            own[pl.ds(bins * depth, wins), :] = mask.astype(jnp.bfloat16)
        src = own.at[cuts[i]]
        if i >= lag:
            settle(*marks[i - lag])
        send(src, rows.at[w, cuts[i]], core_s.at[i], core_r.at[i], dev_core)
        first = len(sent)
        source(i, 0, src)
        marks.append((first, first + 4))
        send(src, rows.at[w, cuts[i]], xrow_s.at[i], xrow_r.at[i], dev_x, rows_first_out)
        copy = pltpu.make_async_copy(src, rows.at[w, cuts[i]], local_s.at[i])
        copy.start()
        locals_.append(copy)

    half = 2 * pieces
    for kk in range(2):
        for i in range(pieces):
            cut = cuts[i]
            u = kk * pieces + i
            if kk == 0:
                arrive(rows.at[mate, cut], core_s.at[i], core_r.at[i])
                source(i, 1, rows.at[mate, cut])

            @pl.when(jnp.logical_not(is_p))
            def _():
                arrive(cols.at[y, s0[kk], cut], up_p.at[u], zp_r.at[u])

            here = cols.at[y, s0[kk], cut]
            along(i, u, kk, here, jnp.logical_not(is_p), True)
            send(here, here, y_s.at[u], y_r.at[u], dev_y, jnp.logical_not(is_p))

            @pl.when(jnp.logical_not(is_q))
            def _():
                arrive(relay.at[kk, cut], up_q.at[u], zq_r.at[u])

            here = relay.at[kk, cut]
            along(i, u, kk, here, jnp.logical_not(is_q), False)
            send(here, cols.at[y, s0[kk], cut], x_s.at[u], x_r.at[u], dev_x, jnp.logical_not(is_q))

            source_z(i, kk, own.at[cut] if kk == 0 else rows.at[mate, cut], True)
            later = jnp.logical_not(rows_first_in)
            first_row, pair_row = rows.at[s1[0], cut], rows.at[s1[1], cut]
            if kk == 0:
                send(own.at[cut], rows.at[w, cut], xrow_s.at[i], xrow_r.at[i], dev_x,
                     jnp.logical_not(rows_first_out))

                @pl.when(rows_first_in)
                def _():
                    arrive(first_row, xrow_s.at[i], xrow_r.at[i])

                send(first_row, first_row, pair_s.at[i], pair_r.at[i], dev_core, rows_first_in)
                here = first_row
            else:
                @pl.when(rows_first_in)
                def _():
                    arrive(pair_row, pair_s.at[i], pair_r.at[i])

                @pl.when(later)
                def _():
                    arrive(first_row, xrow_s.at[i], xrow_r.at[i])

                send(first_row, first_row, pair_s.at[i], pair_r.at[i], dev_core, later)
                here = pair_row
            send(here, cols.at[y, s1[kk], cut], y_s.at[half + u], y_r.at[half + u], dev_y, is_p)

            @pl.when(jnp.logical_not(is_p))
            def _():
                arrive(cols.at[y, s1[kk], cut], x_s.at[u], x_r.at[u])

            here = cols.at[y, s1[kk], cut]
            send(here, here, y_s.at[half + u], y_r.at[half + u], dev_y, jnp.logical_not(is_p))

    for copy in locals_:
        copy.wait()

    @pl.when(is_p)
    def _():
        copy = pltpu.make_async_copy(rows, cols.at[y], local_s.at[pieces])
        copy.start()
        copy.wait()

    for i in range(pieces):
        @pl.when(jnp.logical_not(rows_first_in))
        def _(i=i):
            arrive(rows.at[s1[1], cuts[i]], pair_s.at[i], pair_r.at[i])

    for kk in range(2):
        for i in range(pieces):
            u = kk * pieces + i
            arrive(cols.at[1 - y, s0[kk], cuts[i]], y_s.at[u], y_r.at[u])
            arrive(cols.at[1 - y, s1[kk], cuts[i]], y_s.at[half + u], y_r.at[half + u])

    for entry in sent:
        if entry is None:
            continue
        make, cond = entry
        if cond is None:
            make().wait_send()
        else:
            @pl.when(cond)
            def _(make=make):
                make().wait_send()


def gather_call(spec_re, spec_im, valid, planes):
    bins, wins, width = spec_re.shape
    pieces = bins // 2
    deep = bins * 2 * wins + wins
    sems = lambda n: pltpu.SemaphoreType.DMA((n,))
    u = 2 * pieces
    return pl.pallas_call(
        functools.partial(gather_kernel, bins, wins, pieces, planes),
        out_shape=[
            jax.ShapeDtypeStruct((4, deep, width), jnp.bfloat16),
            jax.ShapeDtypeStruct((2, 4, deep, width), jnp.bfloat16),
            jax.ShapeDtypeStruct((2, deep, width), jnp.bfloat16),
        ],
        in_specs=[pl.BlockSpec(memory_space=pltpu.HBM)] * 3,
        out_specs=[pl.BlockSpec(memory_space=pl.ANY)] * 3,
        scratch_shapes=[
            pltpu.VMEM((bins, wins, width), jnp.bfloat16),
            pltpu.VMEM((bins, wins, width), jnp.bfloat16),
            pltpu.VMEM((wins, width), jnp.int32),
            pltpu.VMEM((deep, width), jnp.bfloat16),
            sems(3),
            sems(pieces), sems(pieces), sems(pieces), sems(pieces), sems(pieces), sems(pieces),
            sems(u), sems(u), sems(u), sems(u), sems(u), sems(u),
            sems(u), sems(u), sems(2 * u), sems(2 * u), sems(pieces + 1),
        ],
        compiler_params=pltpu.CompilerParams(
            collective_id=0, has_side_effects=True, vmem_limit_bytes=16 * 2**20),
    )(spec_re, spec_im, valid)


def spectra_kernel(row_ref, row_mask_ref, col_ref, col_mask_ref, re_ref, im_ref,
                   left_re, left_im, scale, right):
    f, t = pl.program_id(0), pl.program_id(1)
    wins = row_mask_ref.shape[1]
    groups, _, width = row_ref.shape
    halves = col_ref.shape[0]
    depth = groups * 2 * wins

    @pl.when(t == 0)
    def _():
        block = row_ref[...]
        real_part, imag_part = block[:, :wins], block[:, wins:]
        left_re[...] = block.reshape(depth, width).T
        left_im[...] = jnp.concatenate([imag_part, -real_part], 1).reshape(depth, width).T
        for h in range(halves):
            right[:, h * width:(h + 1) * width] = col_ref[h].reshape(depth, width)

    @pl.when((f == 0) & (t == 0))
    def _():
        rows_mask = row_mask_ref[...].reshape(groups * wins, width)
        for h in range(halves):
            cols_mask = col_mask_ref[h].reshape(groups * wins, width)
            count = lax.dot_general(rows_mask, cols_mask, (((0,), (0,)), ((), ())),
                                    preferred_element_type=jnp.float32)
            scale[:, h * width:(h + 1) * width] = 1.0 / jnp.maximum(count, 1.0)

    size = re_ref.shape[1]
    tile = pl.ds(pl.multiple_of(t * size, size), size)
    block = right[...]
    re_ref[0] = jnp.dot(left_re[tile], block, preferred_element_type=jnp.float32) * scale[tile]
    im_ref[0] = jnp.dot(left_im[tile], block, preferred_element_type=jnp.float32) * scale[tile]


def spectra_call(rows, cols, bins, wins):
    groups, _, width = rows.shape
    halves = cols.shape[0]
    depth = groups * 2 * wins
    tiles = 2
    out = jax.ShapeDtypeStruct((bins, width, halves * width), jnp.float32)
    last = 2 * bins
    return pl.pallas_call(
        spectra_kernel,
        grid=(bins, tiles),
        out_shape=[out, out],
        in_specs=[
            pl.BlockSpec((groups, 2 * wins, width), lambda f, t: (0, f, 0)),
            pl.BlockSpec((groups, wins, width), lambda f, t: (0, last, 0)),
            pl.BlockSpec((halves, groups, 2 * wins, width), lambda f, t: (0, 0, f, 0)),
            pl.BlockSpec((halves, groups, wins, width), lambda f, t: (0, 0, last, 0)),
        ],
        out_specs=[pl.BlockSpec((1, width // tiles, halves * width), lambda f, t: (f, t, 0))] * 2,
        scratch_shapes=[
            pltpu.VMEM((width, depth), jnp.bfloat16),
            pltpu.VMEM((width, depth), jnp.bfloat16),
            pltpu.VMEM((width, halves * width), jnp.float32),
            pltpu.VMEM((depth, halves * width), jnp.bfloat16),
        ],
        compiler_params=pltpu.CompilerParams(vmem_limit_bytes=30 * 2**20),
    )(rows, rows, cols, cols)


def on_device_kernels(spec_re, spec_im, valid):
    bins, wins, _ = spec_re.shape
    rows, cols, _ = gather_call(spec_re, spec_im, valid, lax.axis_size("chan") // 2)
    return tuple(spectra_call(rows, cols, bins, wins))


def on_device_general(spec_re, spec_im, valid):
    bins, wins, width = spec_re.shape
    mask = valid.astype(jnp.float32)
    white_re, white_im = whitened(spec_re, spec_im, mask[None])
    mine = jnp.concatenate(
        [white_re.reshape(bins * wins, width), white_im.reshape(bins * wins, width),
         mask.astype(jnp.bfloat16)], 0)
    rows = lax.all_gather(mine, "win")
    groups = rows.shape[0]
    every = lax.all_gather(rows, "chan")
    blocks = every.shape[0] // groups
    cols = lax.dynamic_slice_in_dim(every, lax.axis_index("win") * blocks, blocks, 0)
    cols = jnp.transpose(cols, (1, 2, 0, 3)).reshape(groups, rows.shape[1], blocks * width)

    def split(array):
        n = array.shape[2]
        size = bins * wins
        return (array[:, :size].reshape(groups, bins, wins, n),
                array[:, size:2 * size].reshape(groups, bins, wins, n), array[:, 2 * size:])

    row_re, row_im, row_mask = split(rows)
    col_re, col_im, col_mask = split(cols)
    right = jnp.concatenate([col_re, col_im], 2)

    def product(left):
        return jnp.einsum("gfwi,gfwj->fij", left, right, preferred_element_type=jnp.float32)

    count = jnp.einsum("gwi,gwj->ij", row_mask, col_mask, preferred_element_type=jnp.float32)
    denom = jnp.maximum(count, 1.0)[None]
    total_re = product(jnp.concatenate([row_re, row_im], 2))
    total_im = product(jnp.concatenate([row_im, -row_re], 2))
    return (total_re / denom, total_im / denom)


def solution(mesh):
    fits = mesh.shape["chan"] == 8 and mesh.shape["win"] == 4
    on_device = on_device_kernels if fits else on_device_general
    in_specs = (P(None, "win", "chan"), P(None, "win", "chan"), P("win", "chan"))
    out_specs = (P(None, "chan", "win"), P(None, "chan", "win"))
    return jax.shard_map(
        on_device, mesh=mesh, in_specs=in_specs, out_specs=out_specs, check_vma=False
    )
```
